32 devices in a mesh: expert: 16 (over z, y, x), dp: 2 (over core).
Axes of the slice: x: 2, y: 2, z: 4, core: 2. Of those that a mesh axis runs over, the one named last changes fastest.
Arguments:
- hidden: bfloat16 [4096, 8, 1024], P(('expert', 'dp')), may hold values from -8 to 8
- routes: int32 [4096, 8], P(('expert', 'dp')), may hold values from 0 to 15, as said below
- slots: int32 [4096, 8], P(('expert', 'dp')), may hold values from 0 to 127, as said below
- down_weight: bfloat16 [16, 1024, 7168], P('expert', None, 'dp'), may hold values from -0.1875 to 0.1875
- omega: bfloat16 [16, 1024, 256], P('expert'), may hold values from -0.1875 to 0.1875
Outputs:
- whitening: float32 [16, 1024, 1024], P('expert', 'dp')
- basis: float32 [2, 3584, 256], P('dp', 'expert')
The draws below stay inside these ranges and needn't reach their ends.
Inputs may be any that keep to these rules, and one draw needn't show every extreme that they name: `routes`: each token names 8 different experts. Among the tokens of one device no expert is named more than 128 times, and one expert is named exactly 128 times by the tokens of every device. Among the tokens of one device, the pairs that name one expert have different slots.
All inputs are finite; a program needn't handle non-finite values.
Results may differ from the reference program's by a relative error of at most 0.0032.
Values may be sent and summed in bfloat16 or wider, within the bound.
A program may use at most 128 MiB of HBM per device.

```python
import math
import jax
import jax.numpy as jnp
from jax import lax

D = 7168
TOP = 8
FFW = 1024
R = 256
TOK_DEV = 128
EXPERTS = 16
CAP = 128
TOKENS = 4096
N_DP = 2
DEVICES = 32


def route_table(key):
    hot_expert = jax.random.randint(jax.random.fold_in(key, 7), (), 0, EXPERTS)
    levels = jax.random.randint(jax.random.fold_in(key, 8), (EXPERTS,), 0, 4)
    levels = jnp.where(jnp.arange(EXPERTS) == hot_expert, 12, levels)
    n_cells = EXPERTS * CAP
    n_pairs = TOK_DEV * TOP

    def one_device(dev_index):
        dev_key = jax.random.fold_in(jax.random.fold_in(key, 100), dev_index)
        noise = jax.random.randint(jax.random.fold_in(dev_key, 1), (EXPERTS, CAP), 0, 1024)
        scores = (levels[:, None] * 256 + noise) * n_cells + jnp.arange(n_cells, dtype=jnp.int32).reshape(EXPERTS, CAP)
        picked_vals, picked = lax.top_k(scores.reshape(-1), n_pairs)
        picked = jnp.sort(picked)
        expert_of = picked // CAP
        slot_of = picked % CAP
        position = jnp.arange(n_pairs, dtype=jnp.int32)
        token_perm = jax.random.permutation(jax.random.fold_in(dev_key, 2), TOK_DEV)
        token_of = token_perm[position % TOK_DEV]
        col_keys = jax.random.randint(jax.random.fold_in(dev_key, 3), (TOK_DEV, TOP), 0, 1 << 20) * TOP + jnp.arange(TOP, dtype=jnp.int32)[None, :]
        col_perm = jnp.argsort(col_keys, axis=1).astype(jnp.int32)
        route_of = col_perm[token_of, position // TOK_DEV]
        expert_table = jnp.zeros((TOK_DEV, TOP), jnp.int32).at[token_of, route_of].set(expert_of)
        slot_table = jnp.zeros((TOK_DEV, TOP), jnp.int32).at[token_of, route_of].set(slot_of)
        return (expert_table, slot_table)
    expert_all, slot_all = jax.vmap(one_device)(jnp.arange(DEVICES, dtype=jnp.int32))
    return (expert_all.reshape(TOKENS, TOP), slot_all.reshape(TOKENS, TOP))


def draw_routes(key, part):
    return route_table(key)[0]


def draw_slots(key, part):
    return route_table(key)[1]


def draw_hidden(key, part):
    col_scale = jnp.exp(jax.random.uniform(jax.random.fold_in(key, 11), (FFW,), jnp.float32, jnp.log(0.3), jnp.log(3.0)))
    row_scale = jnp.exp(jax.random.uniform(jax.random.fold_in(key, 12), (TOKENS, TOP, 1), jnp.float32, jnp.log(0.3), jnp.log(3.0)))
    base = jax.random.normal(jax.random.fold_in(key, 13), (TOKENS, TOP, FFW), jnp.float32)
    values = jnp.clip(base * col_scale * row_scale, -8.0, 8.0)
    return values.astype(jnp.bfloat16)


def level_of(key, shape, split, low, largest):
    gain, own = 1.0, jax.random.fold_in(key, 6)
    for dim, blocks in split:
        steps = jnp.exp(jax.random.uniform(jax.random.fold_in(own, dim), (blocks,), jnp.float32, low / len(split), largest / len(split)))
        gain = gain * jnp.repeat(steps, shape[dim] // blocks).reshape([-1 if axis == dim else 1 for axis in range(len(shape))])
    return gain


def gaussian(rng, extent, deviation, limit, cuts=(), kind=jnp.bfloat16):
    array = jax.random.normal(rng, extent, jnp.float32) * deviation
    if len(cuts) > 0:
        array = level_of(rng, extent, cuts, -0.22, 0.18) * array
    return jnp.clip(array, min=-limit, max=limit).astype(kind)


def setup_inputs(seed: int = 0) -> dict:
    arg_keys = jax.random.split(jax.random.key(seed), 6)
    return {
        "hidden": draw_hidden(jax.random.fold_in(arg_keys[5], 71), 0),
        "routes": draw_routes(jax.random.fold_in(arg_keys[5], 71), 0),
        "slots": draw_slots(jax.random.fold_in(arg_keys[5], 71), 0),
        "down_weight": gaussian(arg_keys[3], (EXPERTS, FFW, D), FFW ** -0.5, 0.1875, ((0, 16), (2, 2))),
        "omega": gaussian(arg_keys[4], (EXPERTS, FFW, R), FFW ** -0.5, 0.1875, ((0, 16),)),
    }


damping = 0.1
jitter = 1e-06

def reference(hidden, routes, slots, down_weight, omega):
    n_slot = DEVICES * CAP
    source_dev = (jnp.arange(TOKENS, dtype=jnp.int32) // TOK_DEV).astype(jnp.int32)[:, None]
    slot_index = (routes * n_slot + source_dev * CAP + slots).astype(jnp.int32).reshape(-1)
    buffer = jnp.zeros((EXPERTS * n_slot, FFW), jnp.bfloat16)
    buffer = buffer.at[slot_index].set(hidden.reshape(-1, FFW)).reshape(EXPERTS, n_slot, FFW)
    identity_mat = jnp.eye(FFW, dtype=jnp.float32)

    def per_expert(running, per_items):
        slot_block, down_mat, test_in = per_items
        gram_mat = lax.dot_general(slot_block.astype(jnp.float32), slot_block.astype(jnp.float32), (((0,), (0,)), ((), ())), preferred_element_type=jnp.float32) / n_slot
        damped = gram_mat + (damping * jnp.mean(jnp.diagonal(gram_mat)) + jitter) * identity_mat
        whitening = jnp.linalg.cholesky(damped)
        test_mat = jnp.dot(whitening, test_in.astype(jnp.float32), precision=lax.Precision.HIGHEST).astype(jnp.bfloat16)
        sketch_term = lax.dot_general(down_mat.astype(jnp.float32), test_mat.astype(jnp.float32), (((0,), (0,)), ((), ())), preferred_element_type=jnp.float32)
        return (running + sketch_term, whitening)
    sketch, whitening = lax.scan(per_expert, jnp.zeros((D, R), jnp.float32), (buffer, down_weight, omega))
    small_gram = jnp.dot(sketch.T, sketch, precision=lax.Precision.HIGHEST)
    qr_factor = jnp.linalg.cholesky(small_gram)
    basis_rows = jax.scipy.linalg.solve_triangular(qr_factor, sketch.T, lower=True).T * math.sqrt(D)
    return (whitening, basis_rows.reshape(N_DP, D // N_DP, R))
```

```python
import functools
import math

import jax
import jax.numpy as jnp
from jax import lax
from jax.experimental import pallas as pl
from jax.experimental.pallas import tpu as pltpu
from jax.sharding import PartitionSpec as P

damping = 0.1
jitter = 1e-06
BLK = 128
PANEL = 4
HIGH = lax.Precision.HIGHEST


def contract(left, right):
    return lax.dot_general(
        left, right, (((0,), (0,)), ((), ())), preferred_element_type=jnp.float32
    )


def dot_nt(left, right):
    return lax.dot_general(
        left, right, (((1,), (1,)), ((), ())),
        precision=HIGH, preferred_element_type=jnp.float32,
    )


def factor_block(block):
    tiles = [block[r:r + 8] for r in range(0, BLK, 8)]
    row_id = lax.broadcasted_iota(jnp.int32, (8, BLK), 0)
    lane_id = lax.broadcasted_iota(jnp.int32, (8, BLK), 1)
    inv_tiles = [
        jnp.where(row_id + r == lane_id, 1.0, 0.0).astype(jnp.float32)
        for r in range(0, BLK, 8)
    ]
    n_tile = BLK // 8
    for start in range(0, BLK, PANEL):
        first = start // 8
        off = start % 8
        cols = [
            {t: jnp.broadcast_to(tiles[t][:, start + m:start + m + 1], (8, BLK))
             for t in range(first, n_tile)}
            for m in range(PANEL)
        ]
        rows = [tiles[first][off + m:off + m + 1] for m in range(PANEL)]
        inv_rows = [inv_tiles[first][off + m:off + m + 1] for m in range(PANEL)]
        for m in range(PANEL):
            pivot = cols[m][first][off + m:off + m + 1]
            recip = 1.0 / pivot
            for t in range(first, n_tile):
                cols[m][t] = cols[m][t] * recip
            cols[m][first] = jnp.where(row_id > off + m, cols[m][first], 0.0)
            for n in range(m + 1, PANEL):
                scale = cols[n][first][off + m:off + m + 1]
                ratio = cols[m][first][off + n:off + n + 1]
                for t in range(first, n_tile):
                    cols[n][t] = cols[n][t] - cols[m][t] * scale
                rows[n] = rows[n] - ratio * rows[m]
                inv_rows[n] = inv_rows[n] - ratio * inv_rows[m]
        for t in range(first, n_tile):
            a, b = tiles[t], inv_tiles[t]
            for m in range(PANEL):
                a = a - cols[m][t] * rows[m]
                b = b - cols[m][t] * inv_rows[m]
            tiles[t], inv_tiles[t] = a, b
    upper, inverse = [], []
    for t in range(n_tile):
        diag = row_id + t * 8 == lane_id
        pivots = jnp.sum(jnp.where(diag, tiles[t], 0.0), axis=1, keepdims=True)
        scale = 1.0 / jnp.sqrt(pivots)
        upper.append(jnp.where(row_id + t * 8 <= lane_id, tiles[t] * scale, 0.0))
        inverse.append(inv_tiles[t] * scale)
    return jnp.concatenate(upper, 0).T, jnp.concatenate(inverse, 0)


def diagonal_mask():
    return lax.broadcasted_iota(jnp.int32, (BLK, BLK), 0) == lax.broadcasted_iota(
        jnp.int32, (BLK, BLK), 1
    )


def whiten_kernel(n_slot, top_a, top_b, low_a, low_b, out):
    width = out.shape[0]
    half = width // 2
    n_blk = width // BLK
    scale = 1.0 / n_slot
    out[:half, :half] = (top_a[...] + top_b[...]) * scale
    out[half:, :] = (low_a[...] + low_b[...]) * scale
    eye = diagonal_mask()
    total = jnp.zeros((BLK, BLK), jnp.float32)
    for k in range(n_blk):
        s = slice(k * BLK, (k + 1) * BLK)
        total = total + jnp.where(eye, out[s, s], 0.0)
    mean = jnp.sum(jnp.sum(total, axis=0, keepdims=True), axis=1, keepdims=True) / width
    shift = jnp.where(eye, damping * mean + jitter, 0.0)
    for k in range(n_blk):
        s = slice(k * BLK, (k + 1) * BLK)
        out[s, s] += shift

    @pl.loop(0, n_blk)
    def _(k):
        here = pl.ds(pl.multiple_of(k * BLK, BLK), BLK)
        lower, inverse = factor_block(out[here, here])
        out[here, here] = lower
        for kk in range(n_blk - 1):
            @pl.when(k == kk)
            def _():
                rest = (kk + 1) * BLK
                panel = dot_nt(out[rest:, kk * BLK:rest], inverse)
                out[rest:, kk * BLK:rest] = panel
                for j in range(kk + 1, n_blk):
                    part = panel[j * BLK - rest:]
                    out[j * BLK:, j * BLK:(j + 1) * BLK] -= dot_nt(part, part[:BLK])

    for k in range(n_blk - 1):
        out[k * BLK:(k + 1) * BLK, (k + 1) * BLK:] = jnp.zeros(
            (BLK, width - (k + 1) * BLK), jnp.float32
        )


def basis_kernel(root, gram, sketch, out, work, inv):
    rank = gram.shape[0]
    n_blk = rank // BLK
    work[...] = gram[...]

    @pl.loop(0, n_blk)
    def _(k):
        here = pl.ds(pl.multiple_of(k * BLK, BLK), BLK)
        _, inverse = factor_block(work[here, here])
        inv[here, :] = inverse
        for kk in range(n_blk - 1):
            @pl.when(k == kk)
            def _():
                rest = (kk + 1) * BLK
                panel = dot_nt(work[rest:, kk * BLK:rest], inverse)
                work[rest:, kk * BLK:rest] = panel
                for j in range(kk + 1, n_blk):
                    part = panel[j * BLK - rest:]
                    work[j * BLK:, j * BLK:(j + 1) * BLK] -= dot_nt(part, part[:BLK])

    for k in range(n_blk):
        s = slice(k * BLK, (k + 1) * BLK)
        right = sketch[:, s]
        for j in range(k):
            t = slice(j * BLK, (j + 1) * BLK)
            right = right - dot_nt(out[:, t], work[s, t])
        out[:, s] = dot_nt(right, inv[s, :])
    out[...] = out[...] * root


def whiten(n_slot, top_a, top_b, low_a, low_b):
    width = low_a.shape[1]
    return pl.pallas_call(
        functools.partial(whiten_kernel, n_slot),
        out_shape=jax.ShapeDtypeStruct((width, width), jnp.float32),
        in_specs=[pl.BlockSpec(memory_space=pltpu.VMEM)] * 4,
        out_specs=pl.BlockSpec(memory_space=pltpu.VMEM),
        compiler_params=pltpu.CompilerParams(vmem_limit_bytes=40 * 2**20),
    )(top_a, top_b, low_a, low_b)


def finish(root, gram, sketch):
    rank = gram.shape[0]
    return pl.pallas_call(
        functools.partial(basis_kernel, root),
        out_shape=jax.ShapeDtypeStruct(sketch.shape, jnp.float32),
        in_specs=[pl.BlockSpec(memory_space=pltpu.VMEM)] * 2,
        out_specs=pl.BlockSpec(memory_space=pltpu.VMEM),
        scratch_shapes=[
            pltpu.VMEM((rank, rank), jnp.float32),
            pltpu.VMEM((rank, BLK), jnp.float32),
        ],
        compiler_params=pltpu.CompilerParams(vmem_limit_bytes=32 * 2**20),
    )(gram, sketch)


def local(hidden, routes, slots, down_weight, omega):
    n_exp = lax.axis_size("expert")
    n_dp = lax.axis_size("dp")
    tok_rows, n_route, hid_width = hidden.shape
    capacity = 2 * tok_rows * n_route // n_exp
    n_slot = n_exp * n_dp * capacity
    slot_index = (routes * capacity + slots).reshape(-1)
    outgoing = jnp.zeros((n_exp * capacity, hid_width), jnp.bfloat16)
    outgoing = (
        outgoing.at[slot_index]
        .set(hidden.reshape(-1, hid_width))
        .reshape(n_exp, capacity, hid_width)
    )
    received = lax.all_to_all(outgoing, "expert", split_axis=0, concat_axis=0, tiled=True).reshape(
        n_exp * capacity, hid_width
    )
    half = hid_width // 2
    swap = [(0, 1), (1, 0)]
    low = contract(received[:, half:], received)
    low_other = lax.ppermute(low, "dp", swap)
    top = contract(received[:, :half], received[:, :half])
    top_other = lax.ppermute(top, "dp", swap)
    whitening = whiten(n_slot, top, top_other, low, low_other)
    test_mat = jnp.dot(
        whitening, omega[0].astype(jnp.float32), precision=HIGH
    ).astype(jnp.bfloat16)
    down_half = down_weight[0]
    half_cols = down_half.shape[1]
    sketch = lax.psum_scatter(
        contract(down_half, test_mat), "expert", scatter_dimension=0, tiled=True
    )
    small_gram = lax.psum(
        lax.dot_general(sketch, sketch, (((0,), (0,)), ((), ())), precision=HIGH),
        ("expert", "dp"),
    )
    basis_rows = finish(math.sqrt(half_cols * n_dp), small_gram, sketch)
    own_rows = lax.dynamic_slice_in_dim(
        whitening, lax.axis_index("dp") * (hid_width // n_dp), hid_width // n_dp, 0
    )
    return (own_rows[None], basis_rows[None])


def solution(mesh):
    placed = (
        P(("expert", "dp"), None, None),
        P(("expert", "dp"), None),
        P(("expert", "dp"), None),
        P("expert", None, "dp"),
        P("expert", None, None),
    )
    return jax.shard_map(
        local,
        mesh=mesh,
        in_specs=placed,
        out_specs=(P("expert", "dp", None), P("dp", "expert", None)),
        check_vma=False,
    )
```

```python
import functools
import math

import jax
import jax.numpy as jnp
from jax import lax
from jax.experimental import pallas as pl
from jax.experimental.pallas import tpu as pltpu
from jax.sharding import PartitionSpec as P

damping = 0.1
jitter = 1e-06
BLK = 128
PANEL = 8
HIGH = lax.Precision.HIGHEST


def contract(left, right):
    return lax.dot_general(
        left, right, (((0,), (0,)), ((), ())), preferred_element_type=jnp.float32
    )


def dot_nt(left, right):
    return lax.dot_general(
        left, right, (((1,), (1,)), ((), ())),
        precision=HIGH, preferred_element_type=jnp.float32,
    )


def factor_block(block):
    tiles = [block[r:r + 8] for r in range(0, BLK, 8)]
    row_id = lax.broadcasted_iota(jnp.int32, (8, BLK), 0)
    lane_id = lax.broadcasted_iota(jnp.int32, (8, BLK), 1)
    inv_tiles = [
        jnp.where(row_id + r == lane_id, 1.0, 0.0).astype(jnp.float32)
        for r in range(0, BLK, 8)
    ]
    n_tile = BLK // 8
    for start in range(0, BLK, PANEL):
        first = start // 8
        off = start % 8
        cols = [
            {t: jnp.broadcast_to(tiles[t][:, start + m:start + m + 1], (8, BLK))
             for t in range(first, n_tile)}
            for m in range(PANEL)
        ]
        rows = [tiles[first][off + m:off + m + 1] for m in range(PANEL)]
        inv_rows = [inv_tiles[first][off + m:off + m + 1] for m in range(PANEL)]
        for m in range(PANEL):
            pivot = cols[m][first][off + m:off + m + 1]
            recip = 1.0 / pivot
            for t in range(first, n_tile):
                cols[m][t] = cols[m][t] * recip
            cols[m][first] = jnp.where(row_id > off + m, cols[m][first], 0.0)
            for n in range(m + 1, PANEL):
                scale = cols[n][first][off + m:off + m + 1]
                ratio = cols[m][first][off + n:off + n + 1]
                for t in range(first, n_tile):
                    cols[n][t] = cols[n][t] - cols[m][t] * scale
                rows[n] = rows[n] - ratio * rows[m]
                inv_rows[n] = inv_rows[n] - ratio * inv_rows[m]
        for t in range(first, n_tile):
            a, b = tiles[t], inv_tiles[t]
            for m in range(PANEL):
                a = a - cols[m][t] * rows[m]
                b = b - cols[m][t] * inv_rows[m]
            tiles[t], inv_tiles[t] = a, b
    upper, inverse = [], []
    for t in range(n_tile):
        diag = row_id + t * 8 == lane_id
        pivots = jnp.sum(jnp.where(diag, tiles[t], 0.0), axis=1, keepdims=True)
        scale = 1.0 / jnp.sqrt(pivots)
        upper.append(jnp.where(row_id + t * 8 <= lane_id, tiles[t] * scale, 0.0))
        inverse.append(inv_tiles[t] * scale)
    return jnp.concatenate(upper, 0).T, jnp.concatenate(inverse, 0)


def diagonal_mask():
    return lax.broadcasted_iota(jnp.int32, (BLK, BLK), 0) == lax.broadcasted_iota(
        jnp.int32, (BLK, BLK), 1
    )


def whiten_kernel(n_slot, top_a, top_b, low_a, low_b, out):
    width = out.shape[0]
    half = width // 2
    n_blk = width // BLK
    scale = 1.0 / n_slot
    out[:half, :half] = (top_a[...] + top_b[...]) * scale
    out[half:, :] = (low_a[...] + low_b[...]) * scale
    eye = diagonal_mask()
    total = jnp.zeros((BLK, BLK), jnp.float32)
    for k in range(n_blk):
        s = slice(k * BLK, (k + 1) * BLK)
        total = total + jnp.where(eye, out[s, s], 0.0)
    mean = jnp.sum(jnp.sum(total, axis=0, keepdims=True), axis=1, keepdims=True) / width
    shift = jnp.where(eye, damping * mean + jitter, 0.0)
    for k in range(n_blk):
        s = slice(k * BLK, (k + 1) * BLK)
        out[s, s] += shift

    @pl.loop(0, n_blk)
    def _(k):
        here = pl.ds(pl.multiple_of(k * BLK, BLK), BLK)
        lower, inverse = factor_block(out[here, here])
        out[here, here] = lower
        for kk in range(n_blk - 1):
            @pl.when(k == kk)
            def _():
                rest = (kk + 1) * BLK
                panel = dot_nt(out[rest:, kk * BLK:rest], inverse)
                out[rest:, kk * BLK:rest] = panel
                for j in range(kk + 1, n_blk):
                    part = panel[j * BLK - rest:]
                    out[j * BLK:, j * BLK:(j + 1) * BLK] -= dot_nt(part, part[:BLK])

    for k in range(n_blk - 1):
        out[k * BLK:(k + 1) * BLK, (k + 1) * BLK:] = jnp.zeros(
            (BLK, width - (k + 1) * BLK), jnp.float32
        )


def basis_kernel(root, gram, sketch, out, work, inv):
    rank = gram.shape[0]
    n_blk = rank // BLK
    work[...] = gram[...]

    @pl.loop(0, n_blk)
    def _(k):
        here = pl.ds(pl.multiple_of(k * BLK, BLK), BLK)
        _, inverse = factor_block(work[here, here])
        inv[here, :] = inverse
        for kk in range(n_blk - 1):
            @pl.when(k == kk)
            def _():
                rest = (kk + 1) * BLK
                panel = dot_nt(work[rest:, kk * BLK:rest], inverse)
                work[rest:, kk * BLK:rest] = panel
                for j in range(kk + 1, n_blk):
                    part = panel[j * BLK - rest:]
                    work[j * BLK:, j * BLK:(j + 1) * BLK] -= dot_nt(part, part[:BLK])

    for k in range(n_blk):
        s = slice(k * BLK, (k + 1) * BLK)
        right = sketch[:, s]
        for j in range(k):
            t = slice(j * BLK, (j + 1) * BLK)
            right = right - dot_nt(out[:, t], work[s, t])
        out[:, s] = dot_nt(right, inv[s, :])
    out[...] = out[...] * root


def whiten(n_slot, top_a, top_b, low_a, low_b):
    width = low_a.shape[1]
    return pl.pallas_call(
        functools.partial(whiten_kernel, n_slot),
        out_shape=jax.ShapeDtypeStruct((width, width), jnp.float32),
        in_specs=[pl.BlockSpec(memory_space=pltpu.VMEM)] * 4,
        out_specs=pl.BlockSpec(memory_space=pltpu.VMEM),
        compiler_params=pltpu.CompilerParams(vmem_limit_bytes=40 * 2**20),
    )(top_a, top_b, low_a, low_b)


def finish(root, gram, sketch):
    rank = gram.shape[0]
    return pl.pallas_call(
        functools.partial(basis_kernel, root),
        out_shape=jax.ShapeDtypeStruct(sketch.shape, jnp.float32),
        in_specs=[pl.BlockSpec(memory_space=pltpu.VMEM)] * 2,
        out_specs=pl.BlockSpec(memory_space=pltpu.VMEM),
        scratch_shapes=[
            pltpu.VMEM((rank, rank), jnp.float32),
            pltpu.VMEM((rank, BLK), jnp.float32),
        ],
        compiler_params=pltpu.CompilerParams(vmem_limit_bytes=32 * 2**20),
    )(gram, sketch)


def exchange(parts, bit, axis):
    mine = (lax.axis_index("expert") // bit) % 2
    pairs = [(i, i ^ bit) for i in range(lax.axis_size("expert"))]
    sent = lax.dynamic_index_in_dim(parts, 1 - mine, axis, keepdims=False)
    kept = lax.dynamic_index_in_dim(parts, mine, axis, keepdims=False)
    return kept, lax.ppermute(sent, "expert", pairs)


def scatter_sum(down_half, test_mat, n_exp):
    half_cols = down_half.shape[1]
    share = half_cols // n_exp
    rank = test_mat.shape[1]
    outer = n_exp // 4
    cut = half_cols // 2
    shape = (outer // 2, 2, 2, share, rank)
    first = contract(down_half[:, :cut], test_mat).reshape(shape)
    first_kept, first_came = exchange(first, 1, 2)
    second = contract(down_half[:, cut:], test_mat).reshape(shape)
    second_kept, second_came = exchange(second, 2, 1)
    first = first_kept + first_came
    first_kept, first_came = exchange(first, 2, 1)
    second = second_kept + second_came
    second_kept, second_came = exchange(second, 1, 1)
    quarter = jnp.concatenate([first_kept + first_came, second_kept + second_came], 0)
    groups = [[r + 4 * h for h in range(outer)] for r in range(4)]
    terms = lax.all_to_all(
        quarter, "expert", split_axis=0, concat_axis=0, axis_index_groups=groups, tiled=True
    )
    return jnp.sum(terms, 0)


def gram_over_all(sketch, n_exp, swap):
    rank = sketch.shape[1]
    partial = lax.dot_general(sketch, sketch, (((0,), (0,)), ((), ())), precision=HIGH)
    pieces = partial.reshape(n_exp, rank // n_exp, rank)
    own = jnp.sum(
        lax.all_to_all(pieces, "expert", split_axis=0, concat_axis=0, tiled=True), 0
    )
    own = own + lax.ppermute(own, "dp", swap)
    copies = jnp.broadcast_to(own[None], pieces.shape)
    return lax.all_to_all(
        copies, "expert", split_axis=0, concat_axis=0, tiled=True
    ).reshape(rank, rank)


def local(hidden, routes, slots, down_weight, omega):
    n_exp = lax.axis_size("expert")
    n_dp = lax.axis_size("dp")
    tok_rows, n_route, hid_width = hidden.shape
    capacity = 2 * tok_rows * n_route // n_exp
    n_slot = n_exp * n_dp * capacity
    slot_index = (routes * capacity + slots).reshape(-1)
    outgoing = jnp.zeros((n_exp * capacity, hid_width), jnp.bfloat16)
    outgoing = (
        outgoing.at[slot_index]
        .set(hidden.reshape(-1, hid_width))
        .reshape(n_exp, capacity, hid_width)
    )
    received = lax.all_to_all(outgoing, "expert", split_axis=0, concat_axis=0, tiled=True).reshape(
        n_exp * capacity, hid_width
    )
    half = hid_width // 2
    swap = [(0, 1), (1, 0)]
    low = contract(received[:, half:], received)
    low_other = lax.ppermute(low, "dp", swap)
    top = contract(received[:, :half], received[:, :half])
    top_other = lax.ppermute(top, "dp", swap)
    whitening = whiten(n_slot, top, top_other, low, low_other)
    test_mat = jnp.dot(
        whitening, omega[0].astype(jnp.float32), precision=HIGH
    ).astype(jnp.bfloat16)
    down_half = down_weight[0]
    half_cols = down_half.shape[1]
    sketch = scatter_sum(down_half, test_mat, n_exp)
    small_gram = gram_over_all(sketch, n_exp, swap)
    basis_rows = finish(math.sqrt(half_cols * n_dp), small_gram, sketch)
    own_rows = lax.dynamic_slice_in_dim(
        whitening, lax.axis_index("dp") * (hid_width // n_dp), hid_width // n_dp, 0
    )
    return (own_rows[None], basis_rows[None])


def solution(mesh):
    placed = (
        P(("expert", "dp"), None, None),
        P(("expert", "dp"), None),
        P(("expert", "dp"), None),
        P("expert", None, "dp"),
        P("expert", None, None),
    )
    return jax.shard_map(
        local,
        mesh=mesh,
        in_specs=placed,
        out_specs=(P("expert", "dp", None), P("dp", "expert", None)),
        check_vma=False,
    )
```

```python
import functools
import math

import jax
import jax.numpy as jnp
from jax import lax
from jax.experimental import pallas as pl
from jax.experimental.pallas import tpu as pltpu
from jax.sharding import PartitionSpec as P

damping = 0.1
jitter = 1e-06
BLK = 128
PANEL = 8
HIGH = lax.Precision.HIGHEST


def contract(left, right):
    return lax.dot_general(
        left, right, (((0,), (0,)), ((), ())), preferred_element_type=jnp.float32
    )


def dot_nt(left, right):
    return lax.dot_general(
        left, right, (((1,), (1,)), ((), ())),
        precision=HIGH, preferred_element_type=jnp.float32,
    )


def factor_block(block):
    tiles = [block[r:r + 8] for r in range(0, BLK, 8)]
    row_id = lax.broadcasted_iota(jnp.int32, (8, BLK), 0)
    lane_id = lax.broadcasted_iota(jnp.int32, (8, BLK), 1)
    inv_tiles = [
        jnp.where(row_id + r == lane_id, 1.0, 0.0).astype(jnp.float32)
        for r in range(0, BLK, 8)
    ]
    n_tile = BLK // 8
    for start in range(0, BLK, PANEL):
        first = start // 8
        off = start % 8
        cols = [
            {t: jnp.broadcast_to(tiles[t][:, start + m:start + m + 1], (8, BLK))
             for t in range(first, n_tile)}
            for m in range(PANEL)
        ]
        rows = [tiles[first][off + m:off + m + 1] for m in range(PANEL)]
        inv_rows = [inv_tiles[first][off + m:off + m + 1] for m in range(PANEL)]
        for m in range(PANEL):
            pivot = cols[m][first][off + m:off + m + 1]
            recip = 1.0 / pivot
            for t in range(first, n_tile):
                cols[m][t] = cols[m][t] * recip
            cols[m][first] = jnp.where(row_id > off + m, cols[m][first], 0.0)
            for n in range(m + 1, PANEL):
                scale = cols[n][first][off + m:off + m + 1]
                ratio = cols[m][first][off + n:off + n + 1]
                for t in range(first, n_tile):
                    cols[n][t] = cols[n][t] - cols[m][t] * scale
                rows[n] = rows[n] - ratio * rows[m]
                inv_rows[n] = inv_rows[n] - ratio * inv_rows[m]
        for t in range(first, n_tile):
            a, b = tiles[t], inv_tiles[t]
            for m in range(PANEL):
                a = a - cols[m][t] * rows[m]
                b = b - cols[m][t] * inv_rows[m]
            tiles[t], inv_tiles[t] = a, b
    upper, inverse = [], []
    for t in range(n_tile):
        diag = row_id + t * 8 == lane_id
        pivots = jnp.sum(jnp.where(diag, tiles[t], 0.0), axis=1, keepdims=True)
        scale = 1.0 / jnp.sqrt(pivots)
        upper.append(jnp.where(row_id + t * 8 <= lane_id, tiles[t] * scale, 0.0))
        inverse.append(inv_tiles[t] * scale)
    return jnp.concatenate(upper, 0).T, jnp.concatenate(inverse, 0)


def diagonal_mask():
    return lax.broadcasted_iota(jnp.int32, (BLK, BLK), 0) == lax.broadcasted_iota(
        jnp.int32, (BLK, BLK), 1
    )


def whiten_kernel(n_slot, top_a, top_b, low_a, low_b, out):
    width = out.shape[0]
    half = width // 2
    n_blk = width // BLK
    scale = 1.0 / n_slot
    out[:half, :half] = (top_a[...] + top_b[...]) * scale
    out[half:, :] = (low_a[...] + low_b[...]) * scale
    eye = diagonal_mask()
    total = jnp.zeros((BLK, BLK), jnp.float32)
    for k in range(n_blk):
        s = slice(k * BLK, (k + 1) * BLK)
        total = total + jnp.where(eye, out[s, s], 0.0)
    mean = jnp.sum(jnp.sum(total, axis=0, keepdims=True), axis=1, keepdims=True) / width
    shift = jnp.where(eye, damping * mean + jitter, 0.0)
    for k in range(n_blk):
        s = slice(k * BLK, (k + 1) * BLK)
        out[s, s] += shift

    @pl.loop(0, n_blk)
    def _(k):
        here = pl.ds(pl.multiple_of(k * BLK, BLK), BLK)
        lower, inverse = factor_block(out[here, here])
        out[here, here] = lower
        for kk in range(n_blk - 1):
            @pl.when(k == kk)
            def _():
                rest = (kk + 1) * BLK
                panel = dot_nt(out[rest:, kk * BLK:rest], inverse)
                out[rest:, kk * BLK:rest] = panel
                for j in range(kk + 1, n_blk):
                    part = panel[j * BLK - rest:]
                    out[j * BLK:, j * BLK:(j + 1) * BLK] -= dot_nt(part, part[:BLK])

    for k in range(n_blk - 1):
        out[k * BLK:(k + 1) * BLK, (k + 1) * BLK:] = jnp.zeros(
            (BLK, width - (k + 1) * BLK), jnp.float32
        )


def basis_kernel(root, gram, sketch, out, work, inv):
    rank = gram.shape[0]
    n_blk = rank // BLK
    work[...] = gram[...]

    @pl.loop(0, n_blk)
    def _(k):
        here = pl.ds(pl.multiple_of(k * BLK, BLK), BLK)
        _, inverse = factor_block(work[here, here])
        inv[here, :] = inverse
        for kk in range(n_blk - 1):
            @pl.when(k == kk)
            def _():
                rest = (kk + 1) * BLK
                panel = dot_nt(work[rest:, kk * BLK:rest], inverse)
                work[rest:, kk * BLK:rest] = panel
                for j in range(kk + 1, n_blk):
                    part = panel[j * BLK - rest:]
                    work[j * BLK:, j * BLK:(j + 1) * BLK] -= dot_nt(part, part[:BLK])

    for k in range(n_blk):
        s = slice(k * BLK, (k + 1) * BLK)
        right = sketch[:, s]
        for j in range(k):
            t = slice(j * BLK, (j + 1) * BLK)
            right = right - dot_nt(out[:, t], work[s, t])
        out[:, s] = dot_nt(right, inv[s, :])
    out[...] = out[...] * root


def whiten(n_slot, top_a, top_b, low_a, low_b):
    width = low_a.shape[1]
    return pl.pallas_call(
        functools.partial(whiten_kernel, n_slot),
        out_shape=jax.ShapeDtypeStruct((width, width), jnp.float32),
        in_specs=[pl.BlockSpec(memory_space=pltpu.VMEM)] * 4,
        out_specs=pl.BlockSpec(memory_space=pltpu.VMEM),
        compiler_params=pltpu.CompilerParams(vmem_limit_bytes=40 * 2**20),
    )(top_a, top_b, low_a, low_b)


def finish(root, gram, sketch):
    rank = gram.shape[0]
    return pl.pallas_call(
        functools.partial(basis_kernel, root),
        out_shape=jax.ShapeDtypeStruct(sketch.shape, jnp.float32),
        in_specs=[pl.BlockSpec(memory_space=pltpu.VMEM)] * 2,
        out_specs=pl.BlockSpec(memory_space=pltpu.VMEM),
        scratch_shapes=[
            pltpu.VMEM((rank, rank), jnp.float32),
            pltpu.VMEM((rank, BLK), jnp.float32),
        ],
        compiler_params=pltpu.CompilerParams(vmem_limit_bytes=32 * 2**20),
    )(gram, sketch)


def term_kernel(test_t, down, out):
    out[...] = jnp.dot(test_t[...], down[...], preferred_element_type=jnp.float32).T


def sketch_term(down_half, test_t, begin, rows):
    rank, depth = test_t.shape
    tile = 256
    skip = begin // tile
    return pl.pallas_call(
        term_kernel,
        grid=(rows // tile,),
        out_shape=jax.ShapeDtypeStruct((rows, rank), jnp.float32),
        in_specs=[
            pl.BlockSpec((rank, depth), lambda i: (0, 0)),
            pl.BlockSpec((depth, tile), lambda i: (0, i + skip)),
        ],
        out_specs=pl.BlockSpec((tile, rank), lambda i: (i, 0)),
        cost_estimate=pl.CostEstimate(
            flops=2 * rows * rank * depth,
            bytes_accessed=2 * rows * depth + 4 * rows * rank,
            transcendentals=0,
        ),
        compiler_params=pltpu.CompilerParams(vmem_limit_bytes=16 * 2**20),
    )(test_t, down_half)


def exchange(parts, bit, axis):
    mine = (lax.axis_index("expert") // bit) % 2
    pairs = [(i, i ^ bit) for i in range(lax.axis_size("expert"))]
    sent = lax.dynamic_index_in_dim(parts, 1 - mine, axis, keepdims=False)
    kept = lax.dynamic_index_in_dim(parts, mine, axis, keepdims=False)
    return kept, lax.ppermute(sent, "expert", pairs)


def scatter_sum(down_half, test_t, n_exp):
    half_cols = down_half.shape[1]
    share = half_cols // n_exp
    rank = test_t.shape[0]
    outer = n_exp // 4
    cut = half_cols // 2
    shape = (outer // 2, 2, 2, share, rank)
    first = sketch_term(down_half, test_t, 0, cut).reshape(shape)
    first_kept, first_came = exchange(first, 1, 2)
    second = sketch_term(down_half, test_t, cut, cut).reshape(shape)
    second_kept, second_came = exchange(second, 2, 1)
    first = first_kept + first_came
    first_kept, first_came = exchange(first, 2, 1)
    second = second_kept + second_came
    second_kept, second_came = exchange(second, 1, 1)
    quarter = jnp.concatenate([first_kept + first_came, second_kept + second_came], 0)
    groups = [[r + 4 * h for h in range(outer)] for r in range(4)]
    terms = lax.all_to_all(
        quarter, "expert", split_axis=0, concat_axis=0, axis_index_groups=groups, tiled=True
    )
    return jnp.sum(terms, 0)


def gram_over_all(sketch, n_exp, swap):
    rank = sketch.shape[1]
    partial = lax.dot_general(sketch, sketch, (((0,), (0,)), ((), ())), precision=HIGH)
    pieces = partial.reshape(n_exp, rank // n_exp, rank)
    own = jnp.sum(
        lax.all_to_all(pieces, "expert", split_axis=0, concat_axis=0, tiled=True), 0
    )
    own = own + lax.ppermute(own, "dp", swap)
    copies = jnp.broadcast_to(own[None], pieces.shape)
    return lax.all_to_all(
        copies, "expert", split_axis=0, concat_axis=0, tiled=True
    ).reshape(rank, rank)


def local(hidden, routes, slots, down_weight, omega):
    n_exp = lax.axis_size("expert")
    n_dp = lax.axis_size("dp")
    tok_rows, n_route, hid_width = hidden.shape
    capacity = 2 * tok_rows * n_route // n_exp
    n_slot = n_exp * n_dp * capacity
    slot_index = (routes * capacity + slots).reshape(-1)
    outgoing = jnp.zeros((n_exp * capacity, hid_width), jnp.bfloat16)
    outgoing = (
        outgoing.at[slot_index]
        .set(hidden.reshape(-1, hid_width))
        .reshape(n_exp, capacity, hid_width)
    )
    received = lax.all_to_all(outgoing, "expert", split_axis=0, concat_axis=0, tiled=True).reshape(
        n_exp * capacity, hid_width
    )
    half = hid_width // 2
    swap = [(0, 1), (1, 0)]
    low = contract(received[:, half:], received)
    low_other = lax.ppermute(low, "dp", swap)
    top = contract(received[:, :half], received[:, :half])
    top_other = lax.ppermute(top, "dp", swap)
    whitening = whiten(n_slot, top, top_other, low, low_other)
    test_t = lax.dot_general(
        omega[0].astype(jnp.float32), whitening, (((0,), (1,)), ((), ())), precision=HIGH
    ).astype(jnp.bfloat16)
    down_half = down_weight[0]
    half_cols = down_half.shape[1]
    sketch = scatter_sum(down_half, test_t, n_exp)
    small_gram = gram_over_all(sketch, n_exp, swap)
    basis_rows = finish(math.sqrt(half_cols * n_dp), small_gram, sketch)
    own_rows = lax.dynamic_slice_in_dim(
        whitening, lax.axis_index("dp") * (hid_width // n_dp), hid_width // n_dp, 0
    )
    return (own_rows[None], basis_rows[None])


def solution(mesh):
    placed = (
        P(("expert", "dp"), None, None),
        P(("expert", "dp"), None),
        P(("expert", "dp"), None),
        P("expert", None, "dp"),
        P("expert", None, None),
    )
    return jax.shard_map(
        local,
        mesh=mesh,
        in_specs=placed,
        out_specs=(P("expert", "dp", None), P("dp", "expert", None)),
        check_vma=False,
    )
```
